256 devices in a mesh: row: 4 (over x), col: 8 (over y, z_hi), feat: 8 (over z_lo, core).
Axes of the slice: x: 4, y: 4, z: 8 (z_hi: 2, z_lo: 4; z = z_hi * 4 + z_lo), core: 2. Of those that a mesh axis runs over, the one named last changes fastest.
Arguments:
- features: bfloat16 [32768, 1024], P(('row', 'col'), 'feat'), may hold values from -6 to 6
- degrees: int32 [32768], P(('row', 'col')), may hold values from 1 to 262159, as said below
- tile_values: bfloat16 [4, 8, 256, 128, 128], P('row', 'col'), may hold values from 0 to 1, as said below
- tile_rows: int32 [4, 8, 256], P('row', 'col'), may hold values from 0 to 63
- tile_cols: int32 [4, 8, 256], P('row', 'col'), may hold values from 0 to 31
- tile_count: int32 [4, 8], P('row', 'col'), may hold values from 128 to 256, as said below
Outputs:
- hop_one: bfloat16 [32768, 1024], P(('row', 'col'), 'feat')
- hop_two: bfloat16 [32768, 1024], P(('row', 'col'), 'feat')
- hop_three: bfloat16 [32768, 1024], P(('row', 'col'), 'feat')
The draws below stay inside these ranges and needn't reach their ends.
Inputs may be any that keep to these rules, and one draw needn't show every extreme that they name: `tile_count`: one row block and column set has all 256 slots live in every draw. `tile_values`: every entry is 0 or 1. `degrees`: each node's degree exceeds the number of ones in its row of A; one node in every draw has the largest degree.
All inputs are finite; a program needn't handle non-finite values.
Results may differ from the reference program's by a relative error of at most 0.024.
Values may be sent and summed in bfloat16 or wider, within the bound.
A program may use at most 128 MiB of HBM per device.

```python
import jax
import jax.numpy as jnp
from jax import lax

F = 1024
TILE = 128
PIECE = 1024
HOPS = 3
K_CAP = 256
NODES = 32768
N_ROW = 4
N_COL = 8


def make_values(key):
    value_key = jax.random.fold_in(key, 11)
    picks = jax.random.randint(value_key, (N_ROW, N_COL, K_CAP, TILE, TILE), 0, 32)
    return (picks == 0).astype(jnp.int32)


def make_counts(key):
    count_base = jax.random.fold_in(key, 23)
    count_key, place_key = jax.random.split(count_base)
    counts = jax.random.randint(count_key, (N_ROW * N_COL,), K_CAP // 2, K_CAP + 1)
    full_at = jax.random.randint(place_key, (), 0, N_ROW * N_COL)
    flat_counts = jnp.where(jnp.arange(N_ROW * N_COL) == full_at, K_CAP, counts)
    return flat_counts.reshape(N_ROW, N_COL).astype(jnp.int32)


def make_rows(key):
    row_key = jax.random.fold_in(key, 31)
    return jax.random.randint(row_key, (N_ROW, N_COL, K_CAP), 0, N_COL * PIECE // TILE).astype(jnp.int32)


def draw_tile_values(key, part):
    return make_values(key).astype(jnp.float32).astype(jnp.bfloat16)


def draw_tile_count(key, part):
    return make_counts(key)


def draw_tile_rows(key, part):
    return make_rows(key)


def draw_degrees(key, part):
    values = make_values(key)
    counts = make_counts(key)
    rows = make_rows(key)
    row_tiles = N_COL * PIECE // TILE
    live = (jnp.arange(K_CAP, dtype=jnp.int32)[None, None, :] < counts[:, :, None]).astype(jnp.int32)
    row_sums = jnp.sum(values, axis=4) * live[:, :, :, None]
    segment_ids = jnp.arange(N_ROW, dtype=jnp.int32)[:, None, None] * row_tiles + rows
    inside = jax.ops.segment_sum(row_sums.reshape(-1, TILE), segment_ids.reshape(-1), num_segments=N_ROW * row_tiles)
    outer_key = jax.random.fold_in(key, 41)
    outside = jax.random.randint(outer_key, (N_ROW * N_COL * PIECE,), 1, 16)
    total = inside.reshape(-1) + outside
    hub_key = jax.random.fold_in(key, 43)
    hub_node = jax.random.randint(hub_key, (), 0, N_ROW * N_COL * PIECE)
    largest = N_COL * K_CAP * TILE + 15
    total = jnp.where(jnp.arange(N_ROW * N_COL * PIECE) == hub_node, largest, total)
    return total.astype(jnp.int32)


def plant(array, own_key, smallest, high):
    index_at = [jax.random.randint(jax.random.fold_in(own_key, axis), (), 0, length) for axis, length in enumerate(array.shape)]
    longest = array.shape.index(max(array.shape))
    neighbour = index_at[:longest] + [(index_at[longest] + 1) % array.shape[longest]] + index_at[longest + 1:]
    return array.at[tuple(index_at)].set(smallest).at[tuple(neighbour)].set(high)


def level_of(stream_key, dims, cuts, smallest, high):
    gain = 1.0
    for dim, blocks in cuts:
        draws = jax.random.uniform(jax.random.fold_in(jax.random.fold_in(stream_key, 6), dim), (blocks,), jnp.float32, smallest / len(cuts), high / len(cuts))
        gain = gain * jnp.repeat(jnp.exp(draws), dims[dim] // blocks).reshape((-1,) + (1,) * (len(dims) - 1 - dim))
    return gain


def centred(stream_key, shape, width, limit, cuts=(), held_as=jnp.bfloat16):
    loudness = level_of(stream_key, shape, cuts, -0.22, 0.18) if cuts else 1.0
    entries = jax.random.normal(stream_key, shape, jnp.float32) * width * loudness
    return jnp.minimum(jnp.maximum(entries, -limit), limit).astype(held_as)


def setup_inputs(seed: int = 0) -> dict:
    arg_keys = jax.random.split(jax.random.key(seed), 7)
    return {
        "features": centred(arg_keys[0], (NODES, F), 1.0, 6.0, ((0, 32), (1, 8))),
        "degrees": draw_degrees(jax.random.fold_in(arg_keys[6], 71), 0),
        "tile_values": draw_tile_values(jax.random.fold_in(arg_keys[6], 71), 0),
        "tile_rows": draw_tile_rows(jax.random.fold_in(arg_keys[6], 71), 0),
        "tile_cols": plant(jax.random.randint(arg_keys[4], (N_ROW, N_COL, K_CAP), 0, N_ROW * PIECE // TILE), jax.random.fold_in(arg_keys[4], 1), 0, (N_ROW * PIECE // TILE) - 1).astype(jnp.int32),
        "tile_count": draw_tile_count(jax.random.fold_in(arg_keys[6], 71), 0),
    }


def reference(features, degrees, tile_values, tile_rows, tile_cols, tile_count):
    node_count = features.shape[0]
    feature_width = features.shape[1]
    per_tile = PIECE // TILE
    row_tiles = N_COL * per_tile
    inv_root = lax.rsqrt(degrees.astype(jnp.float32))[:, None]
    slot_ids = jnp.arange(K_CAP, dtype=jnp.int32)
    live_mask = (slot_ids[None, None, :] < tile_count[:, :, None]).astype(jnp.float32)
    current = features
    results = []
    for repeat in range(HOPS):
        scaled = (inv_root * current.astype(jnp.float32)).astype(jnp.bfloat16)
        grid_blocks = scaled.reshape(N_ROW, N_COL, per_tile, TILE, feature_width)

        def row_block(row_index):

            def device_term(running, col_index):
                weights = tile_values[row_index, col_index].astype(jnp.float32) * live_mask[row_index, col_index][:, None, None]
                col_ids = tile_cols[row_index, col_index]
                chosen = grid_blocks[col_ids // per_tile, col_index, col_ids % per_tile].astype(jnp.float32)
                products = jnp.einsum('kij,kjf->kif', weights, chosen)
                added = jax.ops.segment_sum(products, tile_rows[row_index, col_index], num_segments=row_tiles)
                rounded = lax.optimization_barrier(added.astype(jnp.bfloat16)).astype(jnp.float32)
                return (running + rounded, None)
            start_sum = jnp.zeros((row_tiles, TILE, feature_width), jnp.float32)
            running, unused = lax.scan(device_term, start_sum, jnp.arange(N_COL, dtype=jnp.int32))
            return running
        totals = lax.map(row_block, jnp.arange(N_ROW, dtype=jnp.int32))
        current = (inv_root * totals.reshape(node_count, feature_width)).astype(jnp.bfloat16)
        results.append(current)
    return (results[0], results[1], results[2])
```

```python
import functools

import jax
import jax.numpy as jnp
from jax import lax
from jax.experimental import pallas as pl
from jax.experimental.pallas import tpu as pltpu
from jax.sharding import PartitionSpec as P

HOPS = 3
CHUNKS = 2
UNROLL = 32
TILE = 128
MESH = pl.DeviceIdType.MESH
CONTRACT_LAST = (((1,), (1,)), ((), ()))


def task_order(chunks):
    period, z_at, f_at = 25.4, 10.7, 18.0
    timed = []
    for hop in range(HOPS):
        for chunk in range(chunks):
            start = (hop + chunk / chunks) * period
            timed += [(start, "C", hop, chunk), (start + z_at, "Z", hop, chunk), (start + f_at, "F", hop, chunk)]
    return [entry[1:] for entry in sorted(timed)]


def kernel(chunks, pairs, n_row, n_y, per_tile, slot_s, col_s, keep_s, last_s, has_s, feat_ref, deg_ref, tiles_hbm,
           out_a, out_b, out_c, tiles, totals, running, inv, cur, send, recv_y, z_send, z_recv,
           tile_sem, x_send_sem, x_recv_sem, y_send_sem, y_recv_sem, z_send_sem, z_recv_sem, *gathered):
    outs = (out_a, out_b, out_c)
    width = TILE // chunks
    row = lax.axis_index("row")
    col = lax.axis_index("col")
    y, zh = col // 2, lax.rem(col, 2)

    def x_peer(d):
        return {"row": lax.rem(row + d, n_row)}

    def y_peer(d):
        return {"col": lax.rem(y + d, n_y) * 2 + zh}

    z_peer = {"col": y * 2 + (1 - zh)}
    partners = [x_peer(d) for d in range(1, n_row)] + [y_peer(d) for d in range(1, n_y)] + [z_peer]

    barrier = pltpu.get_barrier_semaphore()
    for partner in partners:
        pl.semaphore_signal(barrier, inc=1, device_id=partner, device_id_type=MESH)
    load = pltpu.make_async_copy(tiles_hbm, tiles, tile_sem.at[0])
    load.start()

    def x_buffer(hop, chunk):
        return gathered[hop * chunks + chunk]

    copies = {}

    def start_gather(hop, chunk):
        piece = x_buffer(hop, chunk).at[pl.ds(row * per_tile, per_tile)]
        for d in range(1, n_row):
            at = (hop * chunks + chunk) * (n_row - 1) + d - 1
            copy = pltpu.make_async_remote_copy(
                src_ref=piece, dst_ref=piece, send_sem=x_send_sem.at[at], recv_sem=x_recv_sem.at[at],
                device_id=x_peer(d), device_id_type=MESH)
            copy.start()
            copies["x", hop, chunk, d] = copy

    inv[...] = lax.rsqrt(deg_ref[...].astype(jnp.float32))
    for t in range(per_tile):
        flipped = feat_ref[t * TILE:(t + 1) * TILE, :].astype(jnp.float32).T
        scaled = (flipped * inv[t:t + 1, :]).astype(jnp.bfloat16)
        for chunk in range(chunks):
            x_buffer(0, chunk)[row * per_tile + t] = scaled[chunk * width:(chunk + 1) * width]
    for buffer in gathered:
        buffer[n_row * per_tile] = jnp.zeros((width, TILE), jnp.bfloat16)
    pl.semaphore_wait(barrier, len(partners))
    for chunk in range(chunks):
        start_gather(0, chunk)
    load.wait()

    def product(hop, chunk):
        x = x_buffer(hop, chunk)
        for d in range(1, n_row):
            copies["x", hop, chunk, d].wait_recv()
        running[...] = jnp.zeros_like(running)

        def group(g, carry):
            total = running[...]
            for u in range(UNROLL):
                k = g * UNROLL + u
                left = jnp.concatenate([x[col_s[2 * k]], x[col_s[2 * k + 1]]], axis=1)
                right = jnp.concatenate([tiles[slot_s[2 * k]], tiles[slot_s[2 * k + 1]]], axis=1)
                term = lax.dot_general(left, right, CONTRACT_LAST, preferred_element_type=jnp.float32)
                total = term + total * keep_s[k]
                totals[k] = total
            running[...] = total
            return carry

        lax.fori_loop(0, pairs // UNROLL, group, 0)
        for z in (1, 0):
            for d in list(range(1, n_y)) + [0]:
                piece = lax.rem(y + d, n_y) * 2 + lax.rem(zh + z, 2)
                for t in range(per_tile):
                    i = piece * per_tile + t
                    send[hop, chunk, z, d, t] = (totals[last_s[i]] * has_s[i]).astype(jnp.bfloat16)
                if d:
                    at = ((hop * chunks + chunk) * 2 + z) * (n_y - 1) + d - 1
                    copy = pltpu.make_async_remote_copy(
                        src_ref=send.at[hop, chunk, z, d], dst_ref=recv_y.at[hop, chunk, z, d - 1],
                        send_sem=y_send_sem.at[at], recv_sem=y_recv_sem.at[at],
                        device_id=y_peer(d), device_id_type=MESH)
                    copy.start()
                    copies["y", hop, chunk, z, d] = copy

    def y_sum(hop, chunk, z, t):
        total = send[hop, chunk, z, 0, t].astype(jnp.float32)
        for d in range(1, n_y):
            total = total + recv_y[hop, chunk, z, d - 1, t].astype(jnp.float32)
        return total

    def z_part(hop, chunk):
        for d in range(1, n_y):
            copies["y", hop, chunk, 1, d].wait_recv()
        for t in range(per_tile):
            z_send[hop, chunk, t] = y_sum(hop, chunk, 1, t).astype(jnp.bfloat16)
        at = hop * chunks + chunk
        copy = pltpu.make_async_remote_copy(
            src_ref=z_send.at[hop, chunk], dst_ref=z_recv.at[hop, chunk],
            send_sem=z_send_sem.at[at], recv_sem=z_recv_sem.at[at], device_id=z_peer, device_id_type=MESH)
        copy.start()
        copies["z", hop, chunk] = copy

    def result(hop, chunk):
        for d in range(1, n_y):
            copies["y", hop, chunk, 0, d].wait_recv()
        copies["z", hop, chunk].wait_recv()
        for t in range(per_tile):
            summed = y_sum(hop, chunk, 0, t) + z_recv[hop, chunk, t].astype(jnp.float32)
            root = inv[t:t + 1, :]
            current = (root * summed).astype(jnp.bfloat16)
            cur[hop, t, chunk * width:(chunk + 1) * width, :] = current
            if hop + 1 < HOPS:
                x_buffer(hop + 1, chunk)[row * per_tile + t] = (root * current.astype(jnp.float32)).astype(jnp.bfloat16)
        if hop + 1 < HOPS:
            start_gather(hop + 1, chunk)

    def flip_out(hop):
        for t in range(per_tile):
            outs[hop][t * TILE:(t + 1) * TILE, :] = cur[hop, t].astype(jnp.float32).T.astype(jnp.bfloat16)

    for kind, hop, chunk in task_order(chunks):
        if kind == "C":
            product(hop, chunk)
        elif kind == "Z":
            z_part(hop, chunk)
        else:
            result(hop, chunk)
            if chunk == chunks - 1:
                flip_out(hop)
    for copy in copies.values():
        copy.wait_send()


def plan(rows, cols, count, row_tiles, zero_tile):
    capacity = rows.shape[0]
    places = capacity + row_tiles
    ids = jnp.arange(capacity, dtype=jnp.int32)
    live = ids < count
    one_hot = (rows[:, None] == jnp.arange(row_tiles, dtype=jnp.int32)[None, :]) & live[:, None]
    in_row = jnp.sum(one_hot.astype(jnp.int32), axis=0)
    pairs = (in_row + 1) // 2
    row_ids = jnp.arange(row_tiles)
    first = jnp.sum(jnp.where(row_ids[None, :] < row_ids[:, None], pairs[None, :], 0), axis=1)
    rank = jnp.sum(((rows[:, None] == rows[None, :]) & (ids[None, :] < ids[:, None]) & live[None, :]).astype(jnp.int32), axis=1)
    place = jnp.sum(jnp.where(one_hot, 2 * first[None, :], 0), axis=1) + rank
    here = (place[:, None] == jnp.arange(places, dtype=jnp.int32)[None, :]) & live[:, None]
    slot = jnp.sum(jnp.where(here, ids[:, None], 0), axis=0)
    column = zero_tile + jnp.sum(jnp.where(here, cols[:, None] - zero_tile, 0), axis=0)
    starts = jnp.sum((here & (rank == 0)[:, None]).astype(jnp.int32), axis=0)[::2]
    keep = (1 - starts).astype(jnp.float32)
    last = jnp.maximum(first + pairs - 1, 0)
    has = (pairs > 0).astype(jnp.float32)
    return slot, column, keep, last, has


def per_device(features, degrees, tile_values, tile_rows, tile_cols, tile_count):
    nodes, width = features.shape
    n_row, n_col = lax.axis_size("row"), lax.axis_size("col")
    n_y = n_col // 2
    per_tile = nodes // TILE
    row_tiles = n_col * per_tile
    capacity = tile_values.shape[2]
    pairs = (capacity + row_tiles) // 2
    chunks = CHUNKS
    part = width // chunks
    slot, column, keep, last, has = plan(tile_rows[0, 0], tile_cols[0, 0], tile_count[0, 0], row_tiles, n_row * per_tile)
    smem = pl.BlockSpec(memory_space=pltpu.SMEM)
    vmem = pl.BlockSpec(memory_space=pltpu.VMEM)
    calls = HOPS * chunks
    bf16, f32 = jnp.bfloat16, jnp.float32
    sem = pltpu.SemaphoreType.DMA
    return pl.pallas_call(
        functools.partial(kernel, chunks, pairs, n_row, n_y, per_tile),
        out_shape=[jax.ShapeDtypeStruct((nodes, width), bf16)] * 3,
        in_specs=[smem] * 5 + [vmem, vmem, pl.BlockSpec(memory_space=pl.ANY)],
        out_specs=[vmem] * 3,
        scratch_shapes=[
            pltpu.VMEM((capacity, TILE, TILE), bf16),
            pltpu.VMEM((pairs, part, TILE), f32),
            pltpu.VMEM((part, TILE), f32),
            pltpu.VMEM((per_tile, TILE), f32),
            pltpu.VMEM((HOPS, per_tile, width, TILE), bf16),
            pltpu.VMEM((HOPS, chunks, 2, n_y, per_tile, part, TILE), bf16),
            pltpu.VMEM((HOPS, chunks, 2, n_y - 1, per_tile, part, TILE), bf16),
            pltpu.VMEM((HOPS, chunks, per_tile, part, TILE), bf16),
            pltpu.VMEM((HOPS, chunks, per_tile, part, TILE), bf16),
            sem((1,)),
            sem((calls * (n_row - 1),)), sem((calls * (n_row - 1),)),
            sem((calls * 2 * (n_y - 1),)), sem((calls * 2 * (n_y - 1),)),
            sem((calls,)), sem((calls,)),
        ] + [pltpu.VMEM((n_row * per_tile + 1, part, TILE), bf16)] * calls,
        compiler_params=pltpu.CompilerParams(
            collective_id=0, has_side_effects=True, vmem_limit_bytes=60 * 2**20),
    )(slot, column, keep, last, has, features, degrees.reshape(per_tile, TILE), tile_values[0, 0])


def solution(mesh):
    placed = (
        P(("row", "col"), "feat"),
        P(("row", "col")),
        P("row", "col", None, None, None),
        P("row", "col", None),
        P("row", "col", None),
        P("row", "col"),
    )
    return jax.shard_map(
        per_device,
        mesh=mesh,
        in_specs=placed,
        out_specs=(P(("row", "col"), "feat"),) * 3,
        check_vma=False,
    )
```

```python
import functools

import jax
import jax.numpy as jnp
from jax import lax
from jax.experimental import pallas as pl
from jax.experimental.pallas import tpu as pltpu
from jax.sharding import PartitionSpec as P

HOPS = 3
CHUNKS = 2
GROUPS = 2
UNROLL = 32
TILE = 128
MESH = pl.DeviceIdType.MESH
CONTRACT_LAST = (((1,), (1,)), ((), ()))


def task_order(chunks, groups):
    period, product, side, delay = 26.0, 4.2, 5.4, 1.0
    timed = []
    for hop in range(HOPS):
        for chunk in range(chunks):
            start = (hop + chunk / chunks) * period
            timed.append((start, "C", hop, chunk, 0))
            for g in range(groups):
                sent = start + product + side * (g + 1) / groups + delay
                timed.append((sent, "Z", hop, chunk, g))
                timed.append((sent + side, "F", hop, chunk, g))
    return [entry[1:] for entry in sorted(timed)]


def plan(zero_tile, count_s, rows_ref, cols_ref, ints, floats):
    f32 = jnp.float32
    count = count_s[0, 0]
    capacity = rows_ref.shape[1]
    places = ints.shape[1]
    rows = rows_ref[...].astype(f32)
    rows_down = jnp.broadcast_to(rows, (TILE, capacity)).T
    cols_down = jnp.broadcast_to(cols_ref[...].astype(f32), (TILE, capacity)).T[:, :1]
    down = lax.broadcasted_iota(jnp.int32, (capacity, TILE), 0)
    across = lax.broadcasted_iota(jnp.int32, (capacity, TILE), 1)
    one_hot = jnp.where((rows_down == across.astype(f32)) & (down < count), 1.0, 0.0)
    in_row = jnp.sum(one_hot, axis=0, keepdims=True)
    pairs = ((in_row.astype(jnp.int32) + 1) // 2).astype(f32)
    before = (lax.broadcasted_iota(jnp.int32, (TILE, TILE), 0) < lax.broadcasted_iota(jnp.int32, (TILE, TILE), 1))
    first = jnp.dot(jnp.broadcast_to(pairs, (16, TILE)).astype(jnp.bfloat16), jnp.where(before, 1.0, 0.0).astype(jnp.bfloat16),
                    preferred_element_type=f32)[:1]
    square = (capacity, capacity)
    a = lax.broadcasted_iota(jnp.int32, square, 0)
    b = lax.broadcasted_iota(jnp.int32, square, 1)
    same = (rows_down[:, :1] == jnp.broadcast_to(rows, square)) & (b < a) & (b < count)
    rank = jnp.sum(jnp.where(same, 1.0, 0.0), axis=1, keepdims=True)
    place = jnp.sum(one_hot * (2.0 * first), axis=1, keepdims=True) + rank
    wide = (capacity, places)
    slot_id = lax.broadcasted_iota(jnp.int32, wide, 0)
    place_id = lax.broadcasted_iota(jnp.int32, wide, 1).astype(f32)
    here = (jnp.broadcast_to(place, wide) == place_id) & (slot_id < count)
    slot = jnp.sum(jnp.where(here, slot_id.astype(f32), 0.0), axis=0, keepdims=True)
    column = zero_tile + jnp.sum(jnp.where(here, jnp.broadcast_to(cols_down - zero_tile, wide), 0.0), axis=0, keepdims=True)
    starts = jnp.sum(jnp.where(here, jnp.broadcast_to(jnp.where(rank == 0.0, 1.0, 0.0), wide), 0.0), axis=0, keepdims=True)
    ints[...] = jnp.zeros_like(ints)
    floats[...] = jnp.zeros_like(floats)
    ints[0:1, :] = slot.astype(jnp.int32)
    ints[1:2, :] = column.astype(jnp.int32)
    ints[2:3, :TILE] = jnp.maximum(first + pairs - 1.0, 0.0).astype(jnp.int32)
    floats[0:1, :] = 1.0 - starts
    floats[1:2, :TILE] = jnp.where(pairs > 0.0, 1.0, 0.0)


def kernel(chunks, groups, pairs, n_row, n_y, per_tile, ints, floats, feat_ref, deg_ref, tiles_hbm,
           out_a, out_b, out_c, tiles, totals, running, inv, cur, send, recv_y, z_send, z_recv,
           local_sem, x_send_sem, x_recv_sem, y_send_sem, y_recv_sem, z_send_sem, z_recv_sem,
           *gathered):
    outs = (out_a, out_b, out_c)
    width = TILE // chunks
    each = per_tile // groups
    row = lax.axis_index("row")
    col = lax.axis_index("col")
    y, zh = col // 2, lax.rem(col, 2)

    def x_peer(d):
        return {"row": lax.rem(row + d, n_row)}

    def y_peer(d):
        return {"col": lax.rem(y + d, n_y) * 2 + zh}

    z_peer = {"col": y * 2 + (1 - zh)}
    partners = [x_peer(d) for d in range(1, n_row)] + [y_peer(d) for d in range(1, n_y)] + [z_peer]

    barrier = pltpu.get_barrier_semaphore()
    for partner in partners:
        pl.semaphore_signal(barrier, inc=1, device_id=partner, device_id_type=MESH)
    load = pltpu.make_async_copy(tiles_hbm, tiles, local_sem.at[0])
    load.start()

    def x_buffer(hop, chunk):
        return gathered[hop * chunks + chunk]

    copies = {}

    def remote(name, number, source, target, sems, peer):
        copy = pltpu.make_async_remote_copy(
            src_ref=source, dst_ref=target, send_sem=sems[0].at[number], recv_sem=sems[1].at[number],
            device_id=peer, device_id_type=MESH)
        copy.start()
        copies[name] = copy

    def start_gather(hop, chunk, g):
        piece = x_buffer(hop, chunk).at[pl.ds(row * per_tile + g * each, each)]
        for d in range(1, n_row):
            number = ((hop * chunks + chunk) * groups + g) * (n_row - 1) + d - 1
            remote(("x", hop, chunk, g, d), number, piece, piece, (x_send_sem, x_recv_sem), x_peer(d))

    inv[...] = lax.rsqrt(deg_ref[...].astype(jnp.float32))
    for t in range(per_tile):
        flipped = feat_ref[t * TILE:(t + 1) * TILE, :].astype(jnp.float32).T
        scaled = (flipped * inv[t:t + 1, :]).astype(jnp.bfloat16)
        for chunk in range(chunks):
            x_buffer(0, chunk)[row * per_tile + t] = scaled[chunk * width:(chunk + 1) * width]
    pl.semaphore_wait(barrier, len(partners))
    for chunk in range(chunks):
        for g in range(groups):
            start_gather(0, chunk, g)
    for buffer in gathered:
        buffer[n_row * per_tile] = jnp.zeros((width, TILE), jnp.bfloat16)
    load.wait()

    def product(hop, chunk):
        x = x_buffer(hop, chunk)
        for g in range(groups):
            for d in range(1, n_row):
                copies["x", hop, chunk, g, d].wait_recv()
        running[...] = jnp.zeros_like(running)

        def group(step, carry):
            total = running[...]
            for u in range(UNROLL):
                k = step * UNROLL + u
                left = jnp.concatenate([x[ints[1, 2 * k]], x[ints[1, 2 * k + 1]]], axis=1)
                right = jnp.concatenate([tiles[ints[0, 2 * k]], tiles[ints[0, 2 * k + 1]]], axis=1)
                term = lax.dot_general(left, right, CONTRACT_LAST, preferred_element_type=jnp.float32)
                total = term + total * floats[0, 2 * k]
                totals[k] = total
            running[...] = total
            return carry

        lax.fori_loop(0, pairs // UNROLL, group, 0)
        for z in (1, 0):
            for g in range(groups):
                for d in list(range(1, n_y)) + [0]:
                    piece = lax.rem(y + d, n_y) * 2 + lax.rem(zh + z, 2)
                    for t in range(g * each, (g + 1) * each):
                        i = piece * per_tile + t
                        send[hop, chunk, z, d, t] = (totals[ints[2, i]] * floats[1, i]).astype(jnp.bfloat16)
                    if d:
                        number = (((hop * chunks + chunk) * 2 + z) * groups + g) * (n_y - 1) + d - 1
                        part = pl.ds(g * each, each)
                        remote(("y", hop, chunk, z, g, d), number, send.at[hop, chunk, z, d, part],
                               recv_y.at[hop, chunk, z, d - 1, part], (y_send_sem, y_recv_sem), y_peer(d))

    def y_sum(hop, chunk, z, t):
        total = send[hop, chunk, z, 0, t].astype(jnp.float32)
        for d in range(1, n_y):
            total = total + recv_y[hop, chunk, z, d - 1, t].astype(jnp.float32)
        return total

    def z_part(hop, chunk, g):
        for d in range(1, n_y):
            copies["y", hop, chunk, 1, g, d].wait_recv()
        for t in range(g * each, (g + 1) * each):
            z_send[hop, chunk, t] = y_sum(hop, chunk, 1, t).astype(jnp.bfloat16)
        part = pl.ds(g * each, each)
        remote(("z", hop, chunk, g), (hop * chunks + chunk) * groups + g, z_send.at[hop, chunk, part],
               z_recv.at[hop, chunk, part], (z_send_sem, z_recv_sem), z_peer)

    def result(hop, chunk, g):
        for d in range(1, n_y):
            copies["y", hop, chunk, 0, g, d].wait_recv()
        copies["z", hop, chunk, g].wait_recv()
        for t in range(g * each, (g + 1) * each):
            summed = y_sum(hop, chunk, 0, t) + z_recv[hop, chunk, t].astype(jnp.float32)
            root = inv[t:t + 1, :]
            current = (root * summed).astype(jnp.bfloat16)
            cur[hop, t, chunk * width:(chunk + 1) * width, :] = current
            if hop + 1 < HOPS:
                x_buffer(hop + 1, chunk)[row * per_tile + t] = (root * current.astype(jnp.float32)).astype(jnp.bfloat16)
        if hop + 1 < HOPS:
            start_gather(hop + 1, chunk, g)

    def flip_out(hop, g):
        for t in range(g * each, (g + 1) * each):
            outs[hop][t * TILE:(t + 1) * TILE, :] = cur[hop, t].astype(jnp.float32).T.astype(jnp.bfloat16)

    for kind, hop, chunk, g in task_order(chunks, groups):
        if kind == "C":
            product(hop, chunk)
        elif kind == "Z":
            z_part(hop, chunk, g)
        else:
            result(hop, chunk, g)
            if chunk == chunks - 1:
                flip_out(hop, g)
    for copy in copies.values():
        copy.wait_send()


def hand_on(in_a, in_b, in_c, out_a, out_b, out_c):
    out_a[...] = in_a[...]
    out_b[...] = in_b[...]
    out_c[...] = in_c[...]


def per_device(features, degrees, tile_values, tile_rows, tile_cols, tile_count):
    nodes, width = features.shape
    n_row, n_col = lax.axis_size("row"), lax.axis_size("col")
    n_y = n_col // 2
    per_tile = nodes // TILE
    row_tiles = n_col * per_tile
    capacity = tile_values.shape[2]
    pairs = (capacity + row_tiles) // 2
    chunks = CHUNKS
    part = width // chunks
    groups = GROUPS
    places = -(-2 * pairs // TILE) * TILE
    smem = pl.BlockSpec(memory_space=pltpu.SMEM)
    vmem = pl.BlockSpec(memory_space=pltpu.VMEM)
    anywhere = pl.BlockSpec(memory_space=pl.ANY)
    calls = HOPS * chunks
    bf16, f32 = jnp.bfloat16, jnp.float32
    sem = pltpu.SemaphoreType.DMA
    ints, floats = pl.pallas_call(
        functools.partial(plan, n_row * per_tile),
        out_shape=[jax.ShapeDtypeStruct((8, places), jnp.int32), jax.ShapeDtypeStruct((8, places), f32)],
        in_specs=[smem, vmem, vmem],
        out_specs=[vmem] * 2,
    )(tile_count, tile_rows[0], tile_cols[0])
    results = pl.pallas_call(
        functools.partial(kernel, chunks, groups, pairs, n_row, n_y, per_tile),
        out_shape=[jax.ShapeDtypeStruct((nodes, width), bf16)] * 3,
        in_specs=[smem] * 2 + [vmem] * 2 + [anywhere],
        out_specs=[vmem] * 3,
        scratch_shapes=[
            pltpu.VMEM((capacity, TILE, TILE), bf16),
            pltpu.VMEM((pairs, part, TILE), f32),
            pltpu.VMEM((part, TILE), f32),
            pltpu.VMEM((per_tile, TILE), f32),
            pltpu.VMEM((HOPS, per_tile, width, TILE), bf16),
            pltpu.VMEM((HOPS, chunks, 2, n_y, per_tile, part, TILE), bf16),
            pltpu.VMEM((HOPS, chunks, 2, n_y - 1, per_tile, part, TILE), bf16),
            pltpu.VMEM((HOPS, chunks, per_tile, part, TILE), bf16),
            pltpu.VMEM((HOPS, chunks, per_tile, part, TILE), bf16),
            sem((1,)),
            sem((calls * groups * (n_row - 1),)), sem((calls * groups * (n_row - 1),)),
            sem((calls * 2 * groups * (n_y - 1),)), sem((calls * 2 * groups * (n_y - 1),)),
            sem((calls * groups,)), sem((calls * groups,)),
        ] + [pltpu.VMEM((n_row * per_tile + 1, part, TILE), bf16)] * calls,
        compiler_params=pltpu.CompilerParams(
            collective_id=0, has_side_effects=True, vmem_limit_bytes=60 * 2**20),
    )(ints, floats, features, degrees.reshape(per_tile, TILE), tile_values[0, 0])
    return pl.pallas_call(
        hand_on,
        out_shape=[jax.ShapeDtypeStruct((nodes, width), bf16)] * 3,
        in_specs=[vmem] * 3,
        out_specs=[vmem] * 3,
    )(*results)


def solution(mesh):
    placed = (
        P(("row", "col"), "feat"),
        P(("row", "col")),
        P("row", "col", None, None, None),
        P("row", "col", None),
        P("row", "col", None),
        P("row", "col"),
    )
    return jax.shard_map(
        per_device,
        mesh=mesh,
        in_specs=placed,
        out_specs=(P(("row", "col"), "feat"),) * 3,
        check_vma=False,
    )
```

```python
import functools

import jax
import jax.numpy as jnp
from jax import lax
from jax.experimental import pallas as pl
from jax.experimental.pallas import tpu as pltpu
from jax.sharding import PartitionSpec as P

HOPS = 3
CHUNKS = 2
GROUPS = 2
UNROLL = 80
TILE = 128
MESH = pl.DeviceIdType.MESH
CONTRACT_LAST = (((1,), (1,)), ((), ()))


def task_order(chunks, groups):
    period, product, side, delay = 26.0, 4.2, 5.4, 1.0
    timed = []
    for hop in range(HOPS):
        for chunk in range(chunks):
            start = (hop + chunk / chunks) * period
            timed.append((start, "C", hop, chunk, 0))
            for g in range(groups):
                sent = start + product + side * (g + 1) / groups + delay
                timed.append((sent, "Z", hop, chunk, g))
                timed.append((sent + side, "F", hop, chunk, g))
    return [entry[1:] for entry in sorted(timed)]


def plan(zero_tile, count_s, rows_ref, cols_ref, ints, floats):
    f32 = jnp.float32
    count = count_s[0, 0]
    capacity = rows_ref.shape[1]
    places = ints.shape[1]
    rows = rows_ref[...].astype(f32)
    rows_down = jnp.broadcast_to(rows, (TILE, capacity)).T
    cols_down = jnp.broadcast_to(cols_ref[...].astype(f32), (TILE, capacity)).T[:, :1]
    down = lax.broadcasted_iota(jnp.int32, (capacity, TILE), 0)
    across = lax.broadcasted_iota(jnp.int32, (capacity, TILE), 1)
    one_hot = jnp.where((rows_down == across.astype(f32)) & (down < count), 1.0, 0.0)
    in_row = jnp.sum(one_hot, axis=0, keepdims=True)
    pairs = ((in_row.astype(jnp.int32) + 1) // 2).astype(f32)
    before = (lax.broadcasted_iota(jnp.int32, (TILE, TILE), 0) < lax.broadcasted_iota(jnp.int32, (TILE, TILE), 1))
    first = jnp.dot(jnp.broadcast_to(pairs, (16, TILE)).astype(jnp.bfloat16), jnp.where(before, 1.0, 0.0).astype(jnp.bfloat16),
                    preferred_element_type=f32)[:1]
    square = (capacity, capacity)
    a = lax.broadcasted_iota(jnp.int32, square, 0)
    b = lax.broadcasted_iota(jnp.int32, square, 1)
    same = (rows_down[:, :1] == jnp.broadcast_to(rows, square)) & (b < a) & (b < count)
    rank = jnp.sum(jnp.where(same, 1.0, 0.0), axis=1, keepdims=True)
    place = jnp.sum(one_hot * (2.0 * first), axis=1, keepdims=True) + rank
    wide = (capacity, places)
    slot_id = lax.broadcasted_iota(jnp.int32, wide, 0)
    place_id = lax.broadcasted_iota(jnp.int32, wide, 1).astype(f32)
    here = (jnp.broadcast_to(place, wide) == place_id) & (slot_id < count)
    slot = jnp.sum(jnp.where(here, slot_id.astype(f32), 0.0), axis=0, keepdims=True)
    column = zero_tile + jnp.sum(jnp.where(here, jnp.broadcast_to(cols_down - zero_tile, wide), 0.0), axis=0, keepdims=True)
    starts = jnp.sum(jnp.where(here, jnp.broadcast_to(jnp.where(rank == 0.0, 1.0, 0.0), wide), 0.0), axis=0, keepdims=True)
    ints[...] = jnp.zeros_like(ints)
    floats[...] = jnp.zeros_like(floats)
    ints[0:1, :] = slot.astype(jnp.int32)
    ints[1:2, :] = column.astype(jnp.int32)
    ints[2:3, :TILE] = jnp.maximum(first + pairs - 1.0, 0.0).astype(jnp.int32)
    floats[0:1, :] = 1.0 - starts
    floats[1:2, :TILE] = jnp.where(pairs > 0.0, 1.0, 0.0)


def kernel(chunks, groups, pairs, n_row, n_y, per_tile, ints, floats, feat_ref, deg_ref, tiles_hbm,
           out_a, out_b, out_c, tiles, totals, running, inv, cur, send, recv_y, z_send, z_recv,
           local_sem, turn, x_send_sem, x_recv_sem, y_send_sem, y_recv_sem, z_send_sem, z_recv_sem,
           *gathered):
    outs = (out_a, out_b, out_c)
    width = TILE // chunks
    each = per_tile // groups
    row = lax.axis_index("row")
    col = lax.axis_index("col")
    y, zh = col // 2, lax.rem(col, 2)

    def x_peer(d):
        return {"row": lax.rem(row + d, n_row)}

    def y_peer(d):
        return {"col": lax.rem(y + d, n_y) * 2 + zh}

    z_peer = {"col": y * 2 + (1 - zh)}
    feat = lax.axis_index("feat")
    core = lax.rem(feat, 2)
    core_peer = {"feat": feat + 1 - 2 * core}
    partners = [core_peer] + [x_peer(d) for d in range(1, n_row)] + [y_peer(d) for d in range(1, n_y)] + [z_peer]

    barrier = pltpu.get_barrier_semaphore()
    for partner in partners:
        pl.semaphore_signal(barrier, inc=1, device_id=partner, device_id_type=MESH)
    load = pltpu.make_async_copy(tiles_hbm, tiles, local_sem.at[0])
    load.start()

    def x_buffer(hop, chunk):
        return gathered[hop * chunks + chunk]

    copies = {}

    def remote(name, number, source, target, sems, peer):
        copy = pltpu.make_async_remote_copy(
            src_ref=source, dst_ref=target, send_sem=sems[0].at[number], recv_sem=sems[1].at[number],
            device_id=peer, device_id_type=MESH)
        copy.start()
        copies[name] = copy

    def start_gather(hop, chunk, g):
        piece = x_buffer(hop, chunk).at[pl.ds(row * per_tile + g * each, each)]
        for d in range(1, n_row):
            number = ((hop * chunks + chunk) * groups + g) * (n_row - 1) + d - 1
            remote(("x", hop, chunk, g, d), number, piece, piece, (x_send_sem, x_recv_sem), x_peer(d))

    inv[...] = lax.rsqrt(deg_ref[...].astype(jnp.float32))
    for t in range(per_tile):
        flipped = feat_ref[t * TILE:(t + 1) * TILE, :].astype(jnp.float32).T
        scaled = (flipped * inv[t:t + 1, :]).astype(jnp.bfloat16)
        for chunk in range(chunks):
            x_buffer(0, chunk)[row * per_tile + t] = scaled[chunk * width:(chunk + 1) * width]
    pl.semaphore_wait(barrier, len(partners))

    @pl.when(core == 1)
    def _():
        pl.semaphore_wait(turn, 1)

    for g in range(groups):
        start_gather(0, 0, g)
    for buffer in gathered:
        buffer[n_row * per_tile] = jnp.zeros((width, TILE), jnp.bfloat16)
    load.wait()

    def product(hop, chunk):
        x = x_buffer(hop, chunk)
        for g in range(groups):
            for d in range(1, n_row):
                copies["x", hop, chunk, g, d].wait_recv()
        if hop == 0 and chunk == 0:
            @pl.when(core == 0)
            def _():
                pl.semaphore_signal(turn, inc=1, device_id=core_peer, device_id_type=MESH)
        running[...] = jnp.zeros_like(running)

        def group(step, carry):
            total = running[...]
            for u in range(UNROLL):
                k = step * UNROLL + u
                left = jnp.concatenate([x[ints[1, 2 * k]], x[ints[1, 2 * k + 1]]], axis=1)
                right = jnp.concatenate([tiles[ints[0, 2 * k]], tiles[ints[0, 2 * k + 1]]], axis=1)
                term = lax.dot_general(left, right, CONTRACT_LAST, preferred_element_type=jnp.float32)
                total = term + total * floats[0, 2 * k]
                totals[k] = total
            running[...] = total
            return carry

        lax.fori_loop(0, pairs // UNROLL, group, 0)
        for z in (1, 0):
            for g in range(groups):
                for d in list(range(1, n_y)) + [0]:
                    piece = lax.rem(y + d, n_y) * 2 + lax.rem(zh + z, 2)
                    for t in range(g * each, (g + 1) * each):
                        i = piece * per_tile + t
                        send[hop, chunk, z, d, t] = (totals[ints[2, i]] * floats[1, i]).astype(jnp.bfloat16)
                    if d:
                        number = (((hop * chunks + chunk) * 2 + z) * groups + g) * (n_y - 1) + d - 1
                        part = pl.ds(g * each, each)
                        remote(("y", hop, chunk, z, g, d), number, send.at[hop, chunk, z, d, part],
                               recv_y.at[hop, chunk, z, d - 1, part], (y_send_sem, y_recv_sem), y_peer(d))

        if hop == 0 and chunk + 1 < chunks:
            for g in range(groups):
                start_gather(0, chunk + 1, g)

    def y_sum(hop, chunk, z, t):
        total = send[hop, chunk, z, 0, t].astype(jnp.float32)
        for d in range(1, n_y):
            total = total + recv_y[hop, chunk, z, d - 1, t].astype(jnp.float32)
        return total

    def z_part(hop, chunk, g):
        for d in range(1, n_y):
            copies["y", hop, chunk, 1, g, d].wait_recv()
        for t in range(g * each, (g + 1) * each):
            z_send[hop, chunk, t] = y_sum(hop, chunk, 1, t).astype(jnp.bfloat16)
        part = pl.ds(g * each, each)
        remote(("z", hop, chunk, g), (hop * chunks + chunk) * groups + g, z_send.at[hop, chunk, part],
               z_recv.at[hop, chunk, part], (z_send_sem, z_recv_sem), z_peer)

    def result(hop, chunk, g):
        for d in range(1, n_y):
            copies["y", hop, chunk, 0, g, d].wait_recv()
        copies["z", hop, chunk, g].wait_recv()
        for t in range(g * each, (g + 1) * each):
            summed = y_sum(hop, chunk, 0, t) + z_recv[hop, chunk, t].astype(jnp.float32)
            root = inv[t:t + 1, :]
            current = (root * summed).astype(jnp.bfloat16)
            cur[hop, t, chunk * width:(chunk + 1) * width, :] = current
            if hop + 1 < HOPS:
                x_buffer(hop + 1, chunk)[row * per_tile + t] = (root * current.astype(jnp.float32)).astype(jnp.bfloat16)
        if hop + 1 < HOPS:
            start_gather(hop + 1, chunk, g)

    def flip_out(hop, g):
        for t in range(g * each, (g + 1) * each):
            outs[hop][t * TILE:(t + 1) * TILE, :] = cur[hop, t].astype(jnp.float32).T.astype(jnp.bfloat16)

    for kind, hop, chunk, g in task_order(chunks, groups):
        if kind == "C":
            product(hop, chunk)
        elif kind == "Z":
            z_part(hop, chunk, g)
        else:
            result(hop, chunk, g)
            if chunk == chunks - 1:
                flip_out(hop, g)
    for copy in copies.values():
        copy.wait_send()


def hand_on(in_a, in_b, in_c, out_a, out_b, out_c):
    out_a[...] = in_a[...]
    out_b[...] = in_b[...]
    out_c[...] = in_c[...]


def per_device(features, degrees, tile_values, tile_rows, tile_cols, tile_count):
    nodes, width = features.shape
    n_row, n_col = lax.axis_size("row"), lax.axis_size("col")
    n_y = n_col // 2
    per_tile = nodes // TILE
    row_tiles = n_col * per_tile
    capacity = tile_values.shape[2]
    pairs = (capacity + row_tiles) // 2
    chunks = CHUNKS
    part = width // chunks
    groups = GROUPS
    places = -(-2 * pairs // TILE) * TILE
    smem = pl.BlockSpec(memory_space=pltpu.SMEM)
    vmem = pl.BlockSpec(memory_space=pltpu.VMEM)
    anywhere = pl.BlockSpec(memory_space=pl.ANY)
    calls = HOPS * chunks
    bf16, f32 = jnp.bfloat16, jnp.float32
    sem = pltpu.SemaphoreType.DMA
    ints, floats = pl.pallas_call(
        functools.partial(plan, n_row * per_tile),
        out_shape=[jax.ShapeDtypeStruct((8, places), jnp.int32), jax.ShapeDtypeStruct((8, places), f32)],
        in_specs=[smem, vmem, vmem],
        out_specs=[vmem] * 2,
    )(tile_count, tile_rows[0], tile_cols[0])
    results = pl.pallas_call(
        functools.partial(kernel, chunks, groups, pairs, n_row, n_y, per_tile),
        out_shape=[jax.ShapeDtypeStruct((nodes, width), bf16)] * 3,
        in_specs=[smem] * 2 + [vmem] * 2 + [anywhere],
        out_specs=[vmem] * 3,
        scratch_shapes=[
            pltpu.VMEM((capacity, TILE, TILE), bf16),
            pltpu.VMEM((pairs, part, TILE), f32),
            pltpu.VMEM((part, TILE), f32),
            pltpu.VMEM((per_tile, TILE), f32),
            pltpu.VMEM((HOPS, per_tile, width, TILE), bf16),
            pltpu.VMEM((HOPS, chunks, 2, n_y, per_tile, part, TILE), bf16),
            pltpu.VMEM((HOPS, chunks, 2, n_y - 1, per_tile, part, TILE), bf16),
            pltpu.VMEM((HOPS, chunks, per_tile, part, TILE), bf16),
            pltpu.VMEM((HOPS, chunks, per_tile, part, TILE), bf16),
            sem((1,)), pltpu.SemaphoreType.REGULAR,
            sem((calls * groups * (n_row - 1),)), sem((calls * groups * (n_row - 1),)),
            sem((calls * 2 * groups * (n_y - 1),)), sem((calls * 2 * groups * (n_y - 1),)),
            sem((calls * groups,)), sem((calls * groups,)),
        ] + [pltpu.VMEM((n_row * per_tile + 1, part, TILE), bf16)] * calls,
        compiler_params=pltpu.CompilerParams(
            collective_id=0, has_side_effects=True, vmem_limit_bytes=60 * 2**20),
    )(ints, floats, features, degrees.reshape(per_tile, TILE), tile_values[0, 0])
    return pl.pallas_call(
        hand_on,
        out_shape=[jax.ShapeDtypeStruct((nodes, width), bf16)] * 3,
        in_specs=[vmem] * 3,
        out_specs=[vmem] * 3,
    )(*results)


def solution(mesh):
    placed = (
        P(("row", "col"), "feat"),
        P(("row", "col")),
        P("row", "col", None, None, None),
        P("row", "col", None),
        P("row", "col", None),
        P("row", "col"),
    )
    return jax.shard_map(
        per_device,
        mesh=mesh,
        in_specs=placed,
        out_specs=(P(("row", "col"), "feat"),) * 3,
        check_vma=False,
    )
```
